768 devices in a mesh: rep: 48 (over x, z), shard: 16 (over y, core).
Axes of the slice: x: 4, y: 8, z: 12, core: 2. Of those that a mesh axis runs over, the one named last changes fastest.
Arguments:
- cotangent: bfloat16 [98304, 1024], P(('rep', 'shard')), may hold values from -0.3984375 to 0.3984375
- pooled: bfloat16 [98304, 8, 128], P(('rep', 'shard')), may hold values from -6 to 6
- fm_weight: bfloat16 [64, 1024], replicated, may hold values from -0.1875 to 0.1875
- row_ids: int32 [768, 8, 192], P(('rep', 'shard')), may hold values from 0 to 9215, as said below
- bag_offsets: int32 [768, 8, 128], P(('rep', 'shard')), may hold values from 0 to 191, as said below
- table: float32 [8, 9216, 128], P(None, 'shard'), may hold values from -3 to 3
- accum: float32 [8, 9216], P(None, 'shard'), may hold values from 0.2 to 4
Outputs:
- new_table: float32 [8, 9216, 128], P(None, 'shard')
- new_accum: float32 [8, 9216], P(None, 'shard')
The draws below stay inside these ranges and needn't reach their ends.
Inputs may be any that keep to these rules, and one draw needn't show every extreme that they name: `row_ids`: for each device and table, at most 24 ids have the same value of id // 576, and exactly 24 for one such value. `bag_offsets`: each row starts at 0 and rises by 1 or 2 from one sample to the next; the last bag ends at 192.
All inputs are finite; a program needn't handle non-finite values.
Results may differ from the reference program's by a relative error of at most 0.006.
Values may be sent and summed in bfloat16 or wider, within the bound.
A program may use at most 32 MiB of HBM per device.

```python
import math
import jax
import jax.numpy as jnp
from jax import lax

TBL = 8
E = 128
B_DEV = 128
ROWS_DEV = 576
LOOK = 192
CAP = 24
BATCH = 98304
ROWS = 9216
N_SHARD = 16
DEVICES = 768


def draw_row_ids(key, part):
    key = jax.random.fold_in(key, 11)

    def single(sub, index):
        keys = jax.random.split(sub, 5)
        slots = N_SHARD * CAP
        owner_of = jnp.arange(slots, dtype=jnp.int32) // CAP
        drawn_owner = jax.random.randint(keys[0], (), 0, N_SHARD).astype(jnp.int32)
        full_owner = jnp.where(index == 0, N_SHARD - 1, drawn_owner).astype(jnp.int32)
        score = jax.random.permutation(keys[1], slots).astype(jnp.int32)
        score = score - jnp.where(owner_of == full_owner, slots, 0)
        order = jnp.argsort(score, stable=True)
        chosen = jax.random.permutation(keys[2], owner_of[order[:LOOK]])
        first = jax.random.randint(keys[3], (LOOK,), 0, ROWS_DEV)
        second = jax.random.randint(keys[4], (LOOK,), 0, ROWS_DEV)
        hit = (chosen == full_owner).astype(jnp.int32)
        first_hit = (jnp.cumsum(hit) == 1) & (hit == 1)
        local = jnp.where(first_hit, ROWS_DEV - 1, jnp.minimum(first, second))
        return chosen * ROWS_DEV + local
    keys = jax.random.split(key, DEVICES * TBL)
    indices = jnp.arange(DEVICES * TBL, dtype=jnp.int32)
    return jax.vmap(single)(keys, indices).reshape(DEVICES, TBL, LOOK).astype(jnp.int32)


def draw_bag_offsets(key, part):
    key = jax.random.fold_in(key, 7)

    def single(sub):
        order = jax.random.permutation(sub, B_DEV).astype(jnp.int32)
        lengths = 1 + (order < LOOK - B_DEV).astype(jnp.int32)
        return jnp.cumsum(lengths) - lengths
    keys = jax.random.split(key, DEVICES * TBL)
    return jax.vmap(single)(keys).reshape(DEVICES, TBL, B_DEV).astype(jnp.int32)


def block_levels(stream_key, extent, cuts, smallest, top_value):
    level, own = 1.0, jax.random.fold_in(stream_key, 6)
    for axis_at, parts in cuts:
        steps = jnp.exp(jax.random.uniform(jax.random.fold_in(own, axis_at), (parts,), jnp.float32, smallest / len(cuts), top_value / len(cuts)))
        level = level * jnp.repeat(steps, extent[axis_at] // parts).reshape([-1 if axis == axis_at else 1 for axis in range(len(extent))])
    return level


def bell_draw(stream_key, shape, spread, reach, pieces=(), kind=jnp.bfloat16):
    result = spread * jax.random.normal(stream_key, shape, jnp.float32)
    if pieces:
        result = result * block_levels(stream_key, shape, pieces, -0.22, 0.18)
    return jnp.clip(result, -reach, reach).astype(kind)


def setup_inputs(seed: int = 0) -> dict:
    arg_keys = jax.random.split(jax.random.key(seed), 8)
    return {
        "cotangent": bell_draw(arg_keys[0], (BATCH, TBL * E), 0.05, 0.3984375, ((0, 768),)),
        "pooled": bell_draw(arg_keys[1], (BATCH, TBL, E), 1.0, 6.0, ((0, 768),)),
        "fm_weight": bell_draw(arg_keys[2], (TBL * TBL, TBL * E), (TBL * E) ** -0.5, 0.1875),
        "row_ids": draw_row_ids(jax.random.fold_in(arg_keys[7], 71), 0),
        "bag_offsets": draw_bag_offsets(jax.random.fold_in(arg_keys[7], 71), 0),
        "table": bell_draw(arg_keys[5], (TBL, ROWS, E), 0.5, 3.0, ((1, 16),), jnp.float32),
        "accum": jnp.clip(jnp.exp(math.log(4.0) - 2.9957323 * jax.random.uniform(arg_keys[6], (TBL, ROWS), jnp.float32) ** block_levels(arg_keys[6], (TBL, ROWS), ((1, 16),), -0.2, 0.2)), 0.2, 4.0),
    }


LEARN = 0.5

def fm_backward(cotangent, pooled, fm_weight):
    batch = pooled.shape[0]
    tables = pooled.shape[1]
    width = pooled.shape[2]
    dz = jnp.dot(cotangent, fm_weight.T, preferred_element_type=jnp.float32).reshape(batch, tables, tables)
    symmetric = dz + jnp.swapaxes(dz, 1, 2)
    grad = cotangent.astype(jnp.float32).reshape(batch, tables, width)
    grad = grad + jnp.einsum('bij,bje->bie', symmetric, pooled.astype(jnp.float32))
    return grad.astype(jnp.bfloat16)

def bag_samples(offsets, look):
    position = lax.iota(jnp.int32, look)
    inside = (offsets[:, None, :] <= position[None, :, None]).astype(jnp.int32)
    return lax.optimization_barrier(jnp.sum(inside, axis=2)) - 1

def adagrad(table, accum, grad):
    accum_new = accum + lax.optimization_barrier(jnp.mean(grad * grad, axis=2))
    return (table - LEARN * grad / jnp.sqrt(accum_new)[..., None], accum_new)

def reference(cotangent, pooled, fm_weight, row_ids, bag_offsets, table, accum):
    devices = row_ids.shape[0]
    look = row_ids.shape[2]
    batch_dev = bag_offsets.shape[2]
    rows = table.shape[1]
    table_index = lax.iota(jnp.int32, TBL)[:, None]

    def step(total, index):
        start = (index * batch_dev).astype(jnp.int32)
        cot = lax.dynamic_slice_in_dim(cotangent, start, batch_dev, 0)
        pool = lax.dynamic_slice_in_dim(pooled, start, batch_dev, 0)
        pooled_grad = fm_backward(cot, pool, fm_weight)
        ids = lax.dynamic_index_in_dim(row_ids, index, 0, keepdims=False)
        offsets = lax.dynamic_index_in_dim(bag_offsets, index, 0, keepdims=False)
        sample = bag_samples(offsets, look)
        values = pooled_grad[sample, table_index].astype(jnp.float32)
        return (total.at[table_index, ids].add(values), None)
    start_total = jnp.zeros((TBL, rows, E), jnp.float32)
    grad, _ = lax.scan(step, start_total, jnp.arange(devices, dtype=jnp.int32))
    return adagrad(table, accum, grad)
```

```python
import functools

import jax
import jax.numpy as jnp
from jax import lax
from jax.experimental import pallas as pl
from jax.experimental.pallas import tpu as pltpu
from jax.sharding import PartitionSpec as P

LEARN = 0.5
NX, NZ, NY = 4, 12, 8
GROUPS = 2 * NY
TBL, E, B_DEV, LOOK, CAP, ROWS_DEV = 8, 128, 128, 192, 24, 576
SLOTS = GROUPS * CAP
HEAD = 16
PAIRS = TBL // 2
PAIR_ROWS = 2 * CAP
MSG = HEAD + PAIRS * PAIR_ROWS
HALVES = TBL // NX
CUT = ROWS_DEV // 2
PIECE = ROWS_DEV // NZ
BF, F32, I32 = jnp.bfloat16, jnp.float32, jnp.int32


def iota(shape, dim):
    return lax.broadcasted_iota(I32, shape, dim)


def dot(a, b, dims=((1,), (0,))):
    return lax.dot_general(a, b, (dims, ((), ())), preferred_element_type=F32)


def shard_offsets():
    order = []
    for dy in (4, 3, 5, 2, 6, 1, 7, 0):
        for dc in (0, 1):
            if (dy, dc) != (0, 0):
                order.append((dy, dc))
    return order


def exchange_kernel(
    cot_ref, x_ref, w_ref, ids_ref, off_ref, out_ref,
    send, recv, pg, tgt, dense, relay, relay_out, xin, xsum, zin,
    a2a_s, a2a_r, x1_s, x1_r, x2_s, x2_r, z_s, z_r, zg_s, zg_r, xg_s, xg_r, xf_s, xf_r,
):
    rep = lax.axis_index("rep")
    sh = lax.axis_index("shard")
    mx, mz = rep // NZ, rep % NZ
    my, mc = sh // 2, sh % 2

    def shard_peer(dy, dc):
        return {"rep": rep, "shard": lax.rem(my + dy, NY) * 2 + lax.rem(mc + dc, 2)}

    def x_peer(d):
        return {"rep": lax.rem(mx + d, NX) * NZ + mz, "shard": sh}

    def z_peer(d):
        return {"rep": mx * NZ + lax.rem(mz + d, NZ), "shard": sh}

    barrier = pltpu.get_barrier_semaphore()
    partners = [shard_peer(dy, dc) for dy, dc in shard_offsets()]
    partners += [x_peer(1), x_peer(NX - 1)] + [z_peer(d) for d in range(1, NZ)]
    for peer in partners:
        pl.semaphore_signal(barrier, inc=1, device_id=peer, device_id_type=pl.DeviceIdType.MESH)

    swap = (iota((64, 64), 1) == (iota((64, 64), 0) % 8) * 8 + iota((64, 64), 0) // 8).astype(BF)
    w = w_ref[...]
    w_t = dot(swap, w).astype(BF)
    cot = cot_ref[...]
    sym = dot(cot, w, ((1,), (1,))) + dot(cot, w_t, ((1,), (1,)))
    for i in range(TBL):
        acc = cot_ref[:, i * E:(i + 1) * E].astype(F32)
        for j in range(TBL):
            acc = acc + sym[:, i * TBL + j:i * TBL + j + 1] * x_ref[:, j * E:(j + 1) * E].astype(F32)
        pg[i] = acc.astype(BF)

    ids = ids_ref[...]
    owner = lax.shift_right_logical(ids * 7282, 22)
    local = ids - owner * ROWS_DEV + 1
    rel = ((lax.shift_right_logical(owner, 1) - my) & (NY - 1)) * 2 + ((owner & 1) ^ mc)
    member = jnp.concatenate(
        [(rel[t:t + 1, :] == iota((GROUPS, LOOK), 0)).astype(F32) for t in range(TBL)], axis=0
    )
    earlier = (iota((LOOK, LOOK), 0) < iota((LOOK, LOOK), 1)).astype(BF)
    before = dot(member.astype(BF), earlier)
    rank = jnp.sum((member * before).reshape(TBL, GROUPS, LOOK), axis=1).astype(I32)
    slot = rel * CAP + rank
    high = lax.shift_right_logical(local, 5).astype(F32)
    low = (local & 31).astype(F32)
    after = pltpu.roll(off_ref[...], B_DEV - 1, 1)
    after = jnp.where(iota((TBL, B_DEV), 1) == B_DEV - 1, LOOK, after)

    def spread(t):
        return (iota((SLOTS, LOOK), 0) == slot[t:t + 1, :]).astype(BF)

    rows_h, rows_l = [], []
    for t in range(TBL):
        hl = jnp.where(iota((8, LOOK), 0) == 0, high[t:t + 1, :], low[t:t + 1, :]).astype(BF)
        placed = dot(hl, spread(t), ((1,), (1,)))
        rows_h.append(placed[0:1, :])
        rows_l.append(placed[1:2, :])
    targets = jnp.concatenate(rows_h + rows_l, axis=0)
    mine = (iota((GROUPS, 1, SLOTS), 2) // CAP == iota((GROUPS, 1, SLOTS), 0)).astype(F32)
    fold = (iota((E, SLOTS), 1) % CAP == iota((E, SLOTS), 0)).astype(BF)
    apart = (targets[None] * mine).astype(BF).reshape(GROUPS * HEAD, SLOTS)
    send[:, 0:HEAD, :] = dot(apart, fold, ((1,), (1,))).astype(BF).reshape(GROUPS, HEAD, E)
    recv[0, 0:HEAD, :] = send[0, 0:HEAD, :]

    def a2a(p, dy, dc):
        o = dy * 2 + dc
        first = 0 if p == 0 else HEAD + PAIR_ROWS * p
        rows = pl.ds(first, HEAD + PAIR_ROWS * (p + 1) - first)
        return pltpu.make_async_remote_copy(
            send.at[o, rows], recv.at[o, rows], a2a_s.at[p, o], a2a_r.at[p, o],
            device_id=shard_peer(dy, dc), device_id_type=pl.DeviceIdType.MESH,
        )

    kpos = iota((LOOK, B_DEV), 0)
    sends = []
    for p in range(PAIRS):
        parts = []
        for t in (2 * p, 2 * p + 1):
            bags = ((kpos >= off_ref[t:t + 1, :]) & (kpos < after[t:t + 1, :])).astype(BF)
            values = dot(bags, pg[t]).astype(BF)
            parts.append(dot(spread(t), values).reshape(GROUPS, CAP, E))
        both = jnp.concatenate(parts, axis=1).astype(BF)
        rows = slice(HEAD + PAIR_ROWS * p, HEAD + PAIR_ROWS * (p + 1))
        send[:, rows, :] = both
        recv[0, rows, :] = both[0]
        if p == 0:
            pl.semaphore_wait(barrier, len(partners))
        for dy, dc in shard_offsets():
            copy = a2a(p, dy, dc)
            copy.start()
            sends.append(copy)

    def scatter(p):
        for dy, dc in shard_offsets():
            a2a(p, dy, dc).wait_recv()
        if p == 0:
            heads = dot(recv[:, 0:HEAD, :].reshape(GROUPS * HEAD, E), fold).reshape(GROUPS, HEAD, SLOTS)
            got = jnp.sum(heads * mine, axis=0)
            tgt[...] = (got[0:TBL] * 32.0 + got[TBL:2 * TBL]).astype(I32) - 1
        rows = slice(HEAD + PAIR_ROWS * p, HEAD + PAIR_ROWS * (p + 1))
        both = recv[:, rows, :].astype(F32)
        for a in range(2):
            t = 2 * p + a
            values = both[:, a * CAP:(a + 1) * CAP, :].reshape(SLOTS, E).astype(BF)
            onehot = (iota((ROWS_DEV, SLOTS), 0) == tgt[t:t + 1, :]).astype(BF)
            dense[t] = dot(onehot, values).astype(BF)

    upper, lower = pl.ds(0, CUT), pl.ds(CUT, CUT)

    def table(h, d):
        return h * NX + lax.rem(mx + d, NX)

    def remote(src, dst, s, r, peer):
        return pltpu.make_async_remote_copy(
            src, dst, s, r, device_id=peer, device_id_type=pl.DeviceIdType.MESH
        )

    right, left = x_peer(1), x_peer(NX - 1)

    def x_first(h):
        t2, t1, t3 = table(h, 2), table(h, 1), table(h, 3)
        return [
            remote(dense.at[t2, upper], relay.at[h, 0], x1_s.at[h, 0], x1_r.at[h, 0], right),
            remote(dense.at[t2, lower], relay.at[h, 1], x1_s.at[h, 1], x1_r.at[h, 1], left),
            remote(dense.at[t1, lower], xin.at[h, 0, lower], x1_s.at[h, 2], x1_r.at[h, 2], right),
            remote(dense.at[t3, upper], xin.at[h, 1, upper], x1_s.at[h, 3], x1_r.at[h, 3], left),
        ]

    def x_second(h):
        return [
            remote(relay_out.at[h, 0], xin.at[h, 0, upper], x2_s.at[h, 0], x2_r.at[h, 0], right),
            remote(relay_out.at[h, 1], xin.at[h, 1, lower], x2_s.at[h, 1], x2_r.at[h, 1], left),
        ]

    def z_reduce(h):
        copies = []
        for d in range(1, NZ):
            w_at = lax.rem(mz + d, NZ)
            rows = pl.ds(pl.multiple_of(w_at * PIECE, PIECE), PIECE)
            copies.append(remote(xsum.at[h, rows], zin.at[h, d], z_s.at[h, d], z_r.at[h, d], z_peer(d)))
        return copies

    own_rows = pl.ds(pl.multiple_of(mz * PIECE, PIECE), PIECE)

    def z_gather(h):
        t0 = table(h, 0)
        return [
            remote(out_ref.at[t0, own_rows], out_ref.at[t0, own_rows], zg_s.at[h, d], zg_r.at[h, d], z_peer(d))
            for d in range(1, NZ)
        ]

    def z_gather_wait(h):
        t0 = table(h, 0)
        for d in range(1, NZ):
            at = pl.ds(pl.multiple_of(lax.rem(mz + NZ - d, NZ) * PIECE, PIECE), PIECE)
            remote(out_ref.at[t0, at], out_ref.at[t0, at], zg_s.at[h, d], zg_r.at[h, d], z_peer(d)).wait_recv()

    def x_gather(h, d):
        t0 = table(h, d)
        return [
            remote(out_ref.at[t0, upper], out_ref.at[t0, upper], xg_s.at[h, 0], xg_r.at[h, 0], right),
            remote(out_ref.at[t0, lower], out_ref.at[t0, lower], xg_s.at[h, 1], xg_r.at[h, 1], left),
            remote(out_ref.at[t0, lower], out_ref.at[t0, lower], xg_s.at[h, 2], xg_r.at[h, 2], right),
            remote(out_ref.at[t0, upper], out_ref.at[t0, upper], xg_s.at[h, 3], xg_r.at[h, 3], left),
        ]

    def x_forward(h, d0, d1):
        ta, tb = table(h, d0), table(h, d1)
        return [
            remote(out_ref.at[ta, upper], out_ref.at[ta, upper], xf_s.at[h, 0], xf_r.at[h, 0], right),
            remote(out_ref.at[tb, lower], out_ref.at[tb, lower], xf_s.at[h, 1], xf_r.at[h, 1], left),
        ]

    def start(copies):
        for copy in copies:
            copy.start()
        sends.extend(copies)

    def do_scatter(h):
        for p in range(h * NX // 2, (h + 1) * NX // 2):
            scatter(p)
        start(x_first(h))

    def do_relay(h):
        first, second = x_first(h), x_second(h)
        first[0].wait_recv()
        relay_out[h, 0] = (relay[h, 0].astype(F32) + dense[table(h, 1), upper].astype(F32)).astype(BF)
        start(second[0:1])
        first[1].wait_recv()
        relay_out[h, 1] = (relay[h, 1].astype(F32) + dense[table(h, 3), lower].astype(F32)).astype(BF)
        start(second[1:2])

    def do_x_sum(h):
        first, second = x_first(h), x_second(h)
        for copy in (first[2], first[3], second[0], second[1]):
            copy.wait_recv()
        total = dense[table(h, 0)].astype(F32) + xin[h, 0].astype(F32) + xin[h, 1].astype(F32)
        xsum[h] = total.astype(BF)
        start(z_reduce(h))

    def do_z_sum(h):
        total = xsum[h, own_rows].astype(F32)
        for d, copy in enumerate(z_reduce(h), start=1):
            copy.wait_recv()
            total = total + zin[h, d].astype(F32)
        out_ref[table(h, 0), own_rows] = total.astype(BF)
        start(z_gather(h))

    def do_x_gather(h):
        z_gather_wait(h)
        start(x_gather(h, 0))

    def do_forward(h):
        from_left, from_right = x_gather(h, 3), x_gather(h, 1)
        forward = x_forward(h, 3, 1)
        from_left[0].wait_recv()
        start(forward[0:1])
        from_right[1].wait_recv()
        start(forward[1:2])

    def do_end(h):
        x_gather(h, 3)[2].wait_recv()
        x_gather(h, 1)[3].wait_recv()
        for copy in x_forward(h, 2, 2):
            copy.wait_recv()

    do_scatter(0)
    do_relay(0)
    do_x_sum(0)
    do_scatter(1)
    do_z_sum(0)
    do_relay(1)
    do_x_gather(0)
    do_x_sum(1)
    do_forward(0)
    do_z_sum(1)
    do_end(0)
    do_x_gather(1)
    do_forward(1)
    do_end(1)
    for copy in sends:
        copy.wait_send()


def exchange(cot, pooled, w, ids, offsets):
    vmem = pl.BlockSpec(memory_space=pltpu.VMEM)
    dma = pltpu.SemaphoreType.DMA
    return pl.pallas_call(
        exchange_kernel,
        out_shape=jax.ShapeDtypeStruct((TBL, ROWS_DEV, E), BF),
        in_specs=[vmem] * 5,
        out_specs=vmem,
        scratch_shapes=[
            pltpu.VMEM((GROUPS, MSG, E), BF),
            pltpu.VMEM((GROUPS, MSG, E), BF),
            pltpu.VMEM((TBL, B_DEV, E), BF),
            pltpu.VMEM((TBL, SLOTS), I32),
            pltpu.VMEM((TBL, ROWS_DEV, E), BF),
            pltpu.VMEM((HALVES, 2, CUT, E), BF),
            pltpu.VMEM((HALVES, 2, CUT, E), BF),
            pltpu.VMEM((HALVES, 2, ROWS_DEV, E), BF),
            pltpu.VMEM((HALVES, ROWS_DEV, E), BF),
            pltpu.VMEM((HALVES, NZ, PIECE, E), BF),
            dma((PAIRS, GROUPS)), dma((PAIRS, GROUPS)),
            dma((HALVES, 4)), dma((HALVES, 4)),
            dma((HALVES, 2)), dma((HALVES, 2)),
            dma((HALVES, NZ)), dma((HALVES, NZ)),
            dma((HALVES, NZ)), dma((HALVES, NZ)),
            dma((HALVES, 4)), dma((HALVES, 4)),
            dma((HALVES, 2)), dma((HALVES, 2)),
        ],
        compiler_params=pltpu.CompilerParams(
            collective_id=0, has_side_effects=True, vmem_limit_bytes=40 * 1024 * 1024
        ),
    )(cot, pooled, w, ids, offsets)


def adagrad_kernel(grad_ref, accum_ref, table_hbm, new_table_hbm, new_accum_ref, tab, sem_in, sem_out):
    loads = [pltpu.make_async_copy(table_hbm.at[t], tab.at[t], sem_in.at[t]) for t in range(TBL)]
    stores = [pltpu.make_async_copy(tab.at[t], new_table_hbm.at[t], sem_out.at[t]) for t in range(TBL)]
    for copy in loads:
        copy.start()
    columns = jnp.swapaxes(accum_ref[...], 0, 1)
    fresh = columns
    for t in range(TBL):
        grad = grad_ref[t].astype(F32)
        accum = columns[:, t:t + 1] + jnp.sum(grad * grad, axis=1, keepdims=True) * (1.0 / E)
        fresh = jnp.where(iota((ROWS_DEV, TBL), 1) == t, accum, fresh)
        loads[t].wait()
        tab[t] = tab[t] - grad * (LEARN * lax.rsqrt(accum))
        stores[t].start()
    new_accum_ref[...] = jnp.swapaxes(fresh, 0, 1)
    for copy in stores:
        copy.wait()


def adagrad(grad, accum, table):
    vmem = pl.BlockSpec(memory_space=pltpu.VMEM)
    anywhere = pl.BlockSpec(memory_space=pl.ANY)
    return pl.pallas_call(
        adagrad_kernel,
        out_shape=(
            jax.ShapeDtypeStruct(table.shape, F32),
            jax.ShapeDtypeStruct(accum.shape, F32),
        ),
        in_specs=[vmem, vmem, anywhere],
        out_specs=(anywhere, vmem),
        scratch_shapes=[
            pltpu.VMEM((TBL, ROWS_DEV, E), F32),
            pltpu.SemaphoreType.DMA((TBL,)),
            pltpu.SemaphoreType.DMA((TBL,)),
        ],
        compiler_params=pltpu.CompilerParams(vmem_limit_bytes=40 * 1024 * 1024),
    )(grad, accum, table)


def on_device(cotangent, pooled, fm_weight, row_ids, bag_offsets, table, accum):
    grad = exchange(
        cotangent, pooled.reshape(B_DEV, TBL * E), fm_weight, row_ids[0], bag_offsets[0]
    )
    return adagrad(grad, accum, table)


def solution(mesh):
    return jax.shard_map(
        on_device,
        mesh=mesh,
        in_specs=(
            P(("rep", "shard"), None),
            P(("rep", "shard"), None, None),
            P(),
            P(("rep", "shard"), None, None),
            P(("rep", "shard"), None, None),
            P(None, "shard", None),
            P(None, "shard"),
        ),
        out_specs=(P(None, "shard", None), P(None, "shard")),
        check_vma=False,
    )
```

```python
import jax
import jax.numpy as jnp
from jax import lax
from jax.experimental import pallas as pl
from jax.experimental.pallas import tpu as pltpu
from jax.sharding import PartitionSpec as P

LEARN = 0.5
NX, NZ, NY = 4, 12, 8
GROUPS = 2 * NY
TBL, E, B_DEV, LOOK, CAP, ROWS_DEV = 8, 128, 128, 192, 24, 576
SLOTS = GROUPS * CAP
HEAD = 16
HALVES = TBL // NX
MSG = HALVES * CAP
CHUNKS = ((0, 32), (32, 16))
CUT = ROWS_DEV // 2
PIECE = ROWS_DEV // NZ
BF, F32, I32 = jnp.bfloat16, jnp.float32, jnp.int32
X_ORDER = (2, 1, 3, 0)
Y_ORDER = (4, 3, 5, 2, 6, 1, 7, 0)


def iota(shape, dim):
    return lax.broadcasted_iota(I32, shape, dim)


def dot(a, b, dims=((1,), (0,))):
    return lax.dot_general(a, b, (dims, ((), ())), preferred_element_type=F32)


def group_offsets(own):
    return [(dy, dc) for dy in Y_ORDER for dc in (0, 1) if own or (dy, dc) != (0, 0)]


def remote(src, dst, s, r, peer):
    return pltpu.make_async_remote_copy(
        src, dst, s, r, device_id=peer, device_id_type=pl.DeviceIdType.MESH
    )


def step_kernel(
    cot_hbm, x_hbm, w_hbm, ids_hbm, off_hbm, table_hbm, accum_hbm,
    out_ref, out_accum_ref,
    cot, x_in, x_f, w_v, ids_v, off_v, after_v, slot_v, acc_v, pg,
    head_out, head_in, send, recv, tq, tgt, total, zs, zin, g,
    load_sem, tab_sem, hd_s, hd_r, a_s, a_r, t_s, t_r, z_s, z_r, zg_s, zg_r, xg_s, xg_r, xf_s, xf_r,
):
    rep = lax.axis_index("rep")
    sh = lax.axis_index("shard")
    mx, mz = rep // NZ, rep % NZ
    my, mc = sh // 2, sh % 2

    def peer(dx, dy, dc):
        return {
            "rep": lax.rem(mx + dx, NX) * NZ + mz,
            "shard": lax.rem(my + dy, NY) * 2 + lax.rem(mc + dc, 2),
        }

    def z_peer(d):
        return {"rep": mx * NZ + lax.rem(mz + d, NZ), "shard": sh}

    def a2a_targets(dx):
        return [(dy, dc) for dy, dc in group_offsets(dx != 0)]

    loads = [
        pltpu.make_async_copy(src, dst, load_sem.at[n])
        for n, (src, dst) in enumerate(
            (
                (ids_hbm.at[0], ids_v), (off_hbm.at[0], off_v), (cot_hbm, cot), (w_hbm, w_v),
                (x_hbm, x_in), (accum_hbm, acc_v),
            )
        )
    ]
    for copy in loads:
        copy.start()
    table_load = pltpu.make_async_copy(table_hbm, out_ref, tab_sem)
    table_load.start()

    barrier = pltpu.get_barrier_semaphore()
    partners = [peer(dx, dy, dc) for dx in X_ORDER for dy, dc in a2a_targets(dx)]
    partners += [z_peer(d) for d in range(1, NZ)]
    for other in partners:
        pl.semaphore_signal(barrier, inc=1, device_id=other, device_id_type=pl.DeviceIdType.MESH)
    sends = []

    def start(*copies):
        for copy in copies:
            copy.start()
            sends.append(copy)

    loads[0].wait()
    loads[1].wait()
    ids = ids_v[...]
    owner = lax.shift_right_logical(ids * 7282, 22)
    local = ids - owner * ROWS_DEV + 1
    rel = ((lax.shift_right_logical(owner, 1) - my) & (NY - 1)) * 2 + ((owner & 1) ^ mc)
    member = jnp.concatenate(
        [(rel[t:t + 1, :] == iota((GROUPS, LOOK), 0)).astype(F32) for t in range(TBL)], axis=0
    )
    earlier = (iota((LOOK, LOOK), 0) < iota((LOOK, LOOK), 1)).astype(BF)
    before = dot(member.astype(BF), earlier)
    rank = jnp.sum((member * before).reshape(TBL, GROUPS, LOOK), axis=1).astype(I32)
    slot = rel * CAP + rank
    slot_v[...] = slot
    high = lax.shift_right_logical(local, 5).astype(F32)
    low = (local & 31).astype(F32)
    after = pltpu.roll(off_v[...], B_DEV - 1, 1)
    after_v[...] = jnp.where(iota((TBL, B_DEV), 1) == B_DEV - 1, LOOK, after)

    def spread(row):
        return (iota((SLOTS, LOOK), 0) == row).astype(BF)

    rows_h, rows_l = [], []
    for t in range(TBL):
        hl = jnp.where(iota((8, LOOK), 0) == 0, high[t:t + 1, :], low[t:t + 1, :]).astype(BF)
        placed = dot(hl, spread(slot[t:t + 1, :]), ((1,), (1,)))
        rows_h.append(placed[0:1, :])
        rows_l.append(placed[1:2, :])
    targets = jnp.concatenate(rows_h + rows_l, axis=0)
    mine = (iota((GROUPS, 1, SLOTS), 2) // CAP == iota((GROUPS, 1, SLOTS), 0)).astype(F32)
    fold = (iota((E, SLOTS), 1) % CAP == iota((E, SLOTS), 0)).astype(BF)
    apart = (targets[None] * mine).astype(BF).reshape(GROUPS * HEAD, SLOTS)
    heads = dot(apart, fold, ((1,), (1,))).astype(BF).reshape(GROUPS, HEAD, E)
    head_out[...] = heads
    head_in[0] = heads[0]

    def head_copy(dy, dc):
        o = dy * 2 + dc
        return remote(head_out.at[o], head_in.at[o], hd_s.at[o], hd_r.at[o], peer(0, dy, dc))

    swap = (iota((64, 64), 1) == (iota((64, 64), 0) % 8) * 8 + iota((64, 64), 0) // 8).astype(BF)
    loads[2].wait()
    loads[3].wait()
    w = w_v[...]
    w_t = dot(swap, w).astype(BF)
    sym = dot(cot[...], w, ((1,), (1,))) + dot(cot[...], w_t, ((1,), (1,)))
    loads[4].wait()
    x_f[...] = x_in[...].astype(F32).reshape(B_DEV * TBL, E)
    for i in range(TBL):
        acc = cot[:, i * E:(i + 1) * E].astype(F32)
        for j in range(TBL):
            acc = acc + sym[:, i * TBL + j:i * TBL + j + 1] * x_f[pl.ds(j, B_DEV, stride=TBL), :]
        pg[i] = acc.astype(BF)

    pl.semaphore_wait(barrier, len(partners))
    for dy, dc in group_offsets(False):
        start(head_copy(dy, dc))

    def table(h, d):
        return h * NX + lax.rem(mx + d, NX)

    def a2a(n, dx, dy, dc):
        o = dy * 2 + dc
        rows = pl.ds(*CHUNKS[n])
        return remote(
            send.at[dx, o, rows], recv.at[dx, o, rows], a_s.at[n, dx, o], a_r.at[n, dx, o], peer(dx, dy, dc)
        )

    kpos = iota((LOOK, B_DEV), 0)
    for dx in X_ORDER:
        parts = []
        for h in range(HALVES):
            t = table(h, dx)
            bags = (kpos >= off_v[pl.ds(t, 1), :]) & (kpos < after_v[pl.ds(t, 1), :])
            values = dot(bags.astype(BF), pg[t]).astype(BF)
            parts.append(dot(spread(slot_v[pl.ds(t, 1), :]), values).reshape(GROUPS, CAP, E))
        both = jnp.concatenate(parts, axis=1).astype(BF)
        send[dx] = both
        if dx == 0:
            recv[0, 0] = both[0]
        for dy, dc in a2a_targets(dx):
            start(a2a(0, dx, dy, dc))
    for n in range(1, len(CHUNKS)):
        for dx in X_ORDER:
            for dy, dc in a2a_targets(dx):
                start(a2a(n, dx, dy, dc))

    for dy, dc in group_offsets(False):
        head_copy(dy, dc).wait_recv()
    spots = dot(head_in[...].reshape(GROUPS * HEAD, E), fold).reshape(GROUPS, HEAD, SLOTS)
    got = jnp.sum(spots * mine, axis=0)
    got = got[0:TBL] * 32.0 + got[TBL:2 * TBL] - 1.0
    for q in range(NX):
        tq[q] = jnp.where(iota((8, SLOTS), 0) == 0, got[q:q + 1, :], got[q + NX:q + NX + 1, :])

    def target_copy(dx):
        return remote(tq.at[lax.rem(mx + dx, NX)], tgt.at[dx], t_s.at[dx], t_r.at[dx], peer(dx, 0, 0))

    for dx in X_ORDER[:-1]:
        start(target_copy(dx))
    tgt[0] = tq[mx]

    loads[5].wait()
    order = [(h, d) for h in range(HALVES) for d in range(NX)]
    columns = jnp.swapaxes(
        jnp.concatenate([acc_v[pl.ds(table(h, d), 1), :] for h, d in order], axis=0), 0, 1
    )
    for dx in X_ORDER[:-1]:
        target_copy(dx).wait_recv()

    def scatter(h):
        acc = None
        for dx in X_ORDER:
            for n in range(len(CHUNKS)):
                first = n == h if len(CHUNKS) > 1 else h == 0
                if first:
                    for dy, dc in a2a_targets(dx):
                        a2a(n, dx, dy, dc).wait_recv()
            lo, hi = (0, 32) if h == 0 else (16, 48)
            at = h * CAP - lo
            values = recv[dx, :, lo:hi, :].astype(F32)[:, at:at + CAP, :]
            values = values.reshape(SLOTS, E).astype(BF)
            onehot = (iota((ROWS_DEV, SLOTS), 0) == tgt[dx, h:h + 1, :].astype(I32)).astype(BF)
            part = dot(onehot, values)
            acc = part if acc is None else acc + part
        total[h] = acc
        zs[h] = acc.astype(BF)
        start(*z_reduce(h))

    upper, lower = pl.ds(0, CUT), pl.ds(CUT, CUT)
    right, left = peer(1, 0, 0), peer(NX - 1, 0, 0)
    own_rows = pl.ds(pl.multiple_of(mz * PIECE, PIECE), PIECE)

    def z_rows(d):
        return pl.ds(pl.multiple_of(lax.rem(mz + d, NZ) * PIECE, PIECE), PIECE)

    def z_reduce(h):
        return [
            remote(zs.at[h, z_rows(d)], zin.at[h, d], z_s.at[h, d], z_r.at[h, d], z_peer(d))
            for d in range(1, NZ)
        ]

    def z_gather(h, d, rows):
        at = g.at[table(h, 0), rows]
        return remote(at, at, zg_s.at[h, d], zg_r.at[h, d], z_peer(d))

    def x_gather(h, d, n):
        at = g.at[table(h, d), upper if n in (0, 3) else lower]
        return remote(at, at, xg_s.at[h, n], xg_r.at[h, n], right if n in (0, 2) else left)

    def x_forward(h, d, n):
        at = g.at[table(h, d), lower if n else upper]
        return remote(at, at, xf_s.at[h, n], xf_r.at[h, n], left if n else right)

    def z_sum(h):
        acc = total[h, own_rows]
        for d, copy in enumerate(z_reduce(h), start=1):
            copy.wait_recv()
            acc = acc + zin[h, d].astype(F32)
        g[table(h, 0), own_rows] = acc.astype(BF)
        start(*[z_gather(h, d, own_rows) for d in range(1, NZ)])

    def x_send(h):
        for d in range(1, NZ):
            z_gather(h, d, z_rows(NZ - d)).wait_recv()
        start(*[x_gather(h, 0, n) for n in range(4)])

    fresh = [columns]

    def update(h, d):
        t = table(h, d)
        grad = g[t].astype(F32)
        lane = h * NX + d
        accum = columns[:, lane:lane + 1] + jnp.sum(grad * grad, axis=1, keepdims=True) * (1.0 / E)
        fresh[0] = jnp.where(iota((ROWS_DEV, TBL), 1) == lane, accum, fresh[0])
        out_ref[t] = out_ref[t] - grad * (LEARN * lax.rsqrt(accum))

    def forward(h):
        x_gather(h, 3, 0).wait_recv()
        start(x_forward(h, 3, 0))
        x_gather(h, 1, 1).wait_recv()
        start(x_forward(h, 1, 1))

    def finish(h):
        update(h, 0)
        x_gather(h, 3, 2).wait_recv()
        update(h, 3)
        x_gather(h, 1, 3).wait_recv()
        update(h, 1)
        x_forward(h, 2, 0).wait_recv()
        x_forward(h, 2, 1).wait_recv()
        update(h, 2)

    scatter(0)
    z_sum(0)
    scatter(1)
    x_send(0)
    z_sum(1)
    forward(0)
    x_send(1)
    table_load.wait()
    forward(1)
    finish(0)
    finish(1)
    rows = jnp.swapaxes(fresh[0], 0, 1)
    for n, (h, d) in enumerate(order):
        out_accum_ref[pl.ds(table(h, d), 1), :] = rows[n:n + 1, :]
    for copy in sends:
        copy.wait_send()


def step(cot, pooled, w, ids, offsets, table, accum):
    vmem = pl.BlockSpec(memory_space=pltpu.VMEM)
    anywhere = pl.BlockSpec(memory_space=pl.ANY)
    dma = pltpu.SemaphoreType.DMA
    return pl.pallas_call(
        step_kernel,
        out_shape=(
            jax.ShapeDtypeStruct((TBL, ROWS_DEV, E), F32),
            jax.ShapeDtypeStruct((TBL, ROWS_DEV), F32),
        ),
        in_specs=[anywhere] * 7,
        out_specs=(vmem, vmem),
        scratch_shapes=[
            pltpu.VMEM((B_DEV, TBL * E), BF),
            pltpu.VMEM((B_DEV, TBL, E), BF),
            pltpu.VMEM((B_DEV * TBL, E), F32),
            pltpu.VMEM((TBL * TBL, TBL * E), BF),
            pltpu.VMEM((TBL, LOOK), I32),
            pltpu.VMEM((TBL, B_DEV), I32),
            pltpu.VMEM((TBL, B_DEV), I32),
            pltpu.VMEM((TBL, LOOK), I32),
            pltpu.VMEM((TBL, ROWS_DEV), F32),
            pltpu.VMEM((TBL, B_DEV, E), BF),
            pltpu.VMEM((GROUPS, HEAD, E), BF),
            pltpu.VMEM((GROUPS, HEAD, E), BF),
            pltpu.VMEM((NX, GROUPS, MSG, E), BF),
            pltpu.VMEM((NX, GROUPS, MSG, E), BF),
            pltpu.VMEM((NX, 8, SLOTS), F32),
            pltpu.VMEM((NX, 8, SLOTS), F32),
            pltpu.VMEM((HALVES, ROWS_DEV, E), F32),
            pltpu.VMEM((HALVES, ROWS_DEV, E), BF),
            pltpu.VMEM((HALVES, NZ, PIECE, E), BF),
            pltpu.VMEM((TBL, ROWS_DEV, E), BF),
            dma((6,)), dma,
            dma((GROUPS,)), dma((GROUPS,)),
            dma((len(CHUNKS), NX, GROUPS)), dma((len(CHUNKS), NX, GROUPS)),
            dma((NX,)), dma((NX,)),
            dma((HALVES, NZ)), dma((HALVES, NZ)),
            dma((HALVES, NZ)), dma((HALVES, NZ)),
            dma((HALVES, 4)), dma((HALVES, 4)),
            dma((HALVES, 2)), dma((HALVES, 2)),
        ],
        compiler_params=pltpu.CompilerParams(
            collective_id=0, has_side_effects=True, vmem_limit_bytes=56 * 1024 * 1024
        ),
    )(cot, pooled, w, ids, offsets, table, accum)


def solution(mesh):
    return jax.shard_map(
        step,
        mesh=mesh,
        in_specs=(
            P(("rep", "shard"), None),
            P(("rep", "shard"), None, None),
            P(),
            P(("rep", "shard"), None, None),
            P(("rep", "shard"), None, None),
            P(None, "shard", None),
            P(None, "shard"),
        ),
        out_specs=(P(None, "shard", None), P(None, "shard")),
        check_vma=False,
    )
```

```python
import jax
import jax.numpy as jnp
from jax import lax
from jax.experimental import pallas as pl
from jax.experimental.pallas import tpu as pltpu
from jax.sharding import PartitionSpec as P

LEARN = 0.5
NX, NZ, NY = 4, 12, 8
GROUPS = 2 * NY
TBL, E, B_DEV, LOOK, CAP, ROWS_DEV = 8, 128, 128, 192, 24, 576
SLOTS = GROUPS * CAP
HEAD = 16
HALVES = TBL // NX
MSG = HALVES * CAP
CHUNKS = ((0, 32), (32, 16))
PIECE = ROWS_DEV // NZ
BF, F32, I32 = jnp.bfloat16, jnp.float32, jnp.int32
X_ORDER = (2, 1, 3, 0)
Y_ORDER = (4, 3, 5, 2, 6, 1, 7, 0)
Z_ORDER = (6, 5, 7, 4, 8, 3, 9, 2, 10, 1, 11)
PARTS = ((0, 1), (1, 3), (9, 3), (4, 5))


def iota(shape, dim):
    return lax.broadcasted_iota(I32, shape, dim)


def dot(a, b, dims=((1,), (0,))):
    return lax.dot_general(a, b, (dims, ((), ())), preferred_element_type=F32)


def group_offsets(own):
    return [(dy, dc) for dy in Y_ORDER for dc in (0, 1) if own or (dy, dc) != (0, 0)]


def remote(src, dst, s, r, peer):
    return pltpu.make_async_remote_copy(
        src, dst, s, r, device_id=peer, device_id_type=pl.DeviceIdType.MESH
    )


def step_kernel(
    cot_hbm, x_hbm, w_hbm, ids_hbm, off_hbm, accum_hbm,
    out_ref, out_accum_ref,
    cot, x_in, x_f, w_v, ids_v, off_v, after_v, slot_v, acc_v, pg,
    head_out, head_in, send, recv, tq, tgt, total, zs, zin, g,
    load_sem, hd_s, hd_r, a_s, a_r, t_s, t_r, z_s, z_r, zg_s, zg_r, xg_s, xg_r,
):
    rep = lax.axis_index("rep")
    sh = lax.axis_index("shard")
    mx, mz = rep // NZ, rep % NZ
    my, mc = sh // 2, sh % 2

    def peer(dx, dy, dc):
        return {
            "rep": lax.rem(mx + dx, NX) * NZ + mz,
            "shard": lax.rem(my + dy, NY) * 2 + lax.rem(mc + dc, 2),
        }

    def z_peer(d):
        return {"rep": mx * NZ + lax.rem(mz + d, NZ), "shard": sh}

    def a2a_targets(dx):
        return [(dy, dc) for dy, dc in group_offsets(dx != 0)]

    loads = [
        pltpu.make_async_copy(src, dst, load_sem.at[n])
        for n, (src, dst) in enumerate(
            (
                (ids_hbm.at[0], ids_v), (off_hbm.at[0], off_v), (cot_hbm, cot), (w_hbm, w_v),
                (x_hbm, x_in), (accum_hbm, acc_v),
            )
        )
    ]
    for copy in loads:
        copy.start()

    barrier = pltpu.get_barrier_semaphore()
    partners = [peer(dx, dy, dc) for dx in X_ORDER for dy, dc in a2a_targets(dx)]
    partners += [z_peer(d) for d in range(1, NZ)]
    for other in partners:
        pl.semaphore_signal(barrier, inc=1, device_id=other, device_id_type=pl.DeviceIdType.MESH)
    sends = []

    def start(*copies):
        for copy in copies:
            copy.start()
            sends.append(copy)

    loads[0].wait()
    loads[1].wait()
    ids = ids_v[...]
    owner = lax.shift_right_logical(ids * 7282, 22)
    local = ids - owner * ROWS_DEV + 1
    rel = ((lax.shift_right_logical(owner, 1) - my) & (NY - 1)) * 2 + ((owner & 1) ^ mc)
    member = jnp.concatenate(
        [(rel[t:t + 1, :] == iota((GROUPS, LOOK), 0)).astype(F32) for t in range(TBL)], axis=0
    )
    earlier = (iota((LOOK, LOOK), 0) < iota((LOOK, LOOK), 1)).astype(BF)
    before = dot(member.astype(BF), earlier)
    rank = jnp.sum((member * before).reshape(TBL, GROUPS, LOOK), axis=1).astype(I32)
    slot = rel * CAP + rank
    slot_v[...] = slot
    high = lax.shift_right_logical(local, 5).astype(F32)
    low = (local & 31).astype(F32)
    after = pltpu.roll(off_v[...], B_DEV - 1, 1)
    after_v[...] = jnp.where(iota((TBL, B_DEV), 1) == B_DEV - 1, LOOK, after)

    def spread(row):
        return (iota((SLOTS, LOOK), 0) == row).astype(BF)

    rows_h, rows_l = [], []
    for t in range(TBL):
        hl = jnp.where(iota((8, LOOK), 0) == 0, high[t:t + 1, :], low[t:t + 1, :]).astype(BF)
        placed = dot(hl, spread(slot[t:t + 1, :]), ((1,), (1,)))
        rows_h.append(placed[0:1, :])
        rows_l.append(placed[1:2, :])
    targets = jnp.concatenate(rows_h + rows_l, axis=0)
    mine = (iota((GROUPS, 1, SLOTS), 2) // CAP == iota((GROUPS, 1, SLOTS), 0)).astype(F32)
    fold = (iota((E, SLOTS), 1) % CAP == iota((E, SLOTS), 0)).astype(BF)
    apart = (targets[None] * mine).astype(BF).reshape(GROUPS * HEAD, SLOTS)
    heads = dot(apart, fold, ((1,), (1,))).astype(BF).reshape(GROUPS, HEAD, E)
    head_out[...] = heads
    head_in[0] = heads[0]

    def head_copy(dy, dc):
        o = dy * 2 + dc
        return remote(head_out.at[o], head_in.at[o], hd_s.at[o], hd_r.at[o], peer(0, dy, dc))

    swap = (iota((64, 64), 1) == (iota((64, 64), 0) % 8) * 8 + iota((64, 64), 0) // 8).astype(BF)
    loads[2].wait()
    loads[3].wait()
    w = w_v[...]
    w_t = dot(swap, w).astype(BF)
    sym = dot(cot[...], w, ((1,), (1,))) + dot(cot[...], w_t, ((1,), (1,)))
    loads[4].wait()
    x_f[...] = x_in[...].astype(F32).reshape(B_DEV * TBL, E)
    for i in range(TBL):
        acc = cot[:, i * E:(i + 1) * E].astype(F32)
        for j in range(TBL):
            acc = acc + sym[:, i * TBL + j:i * TBL + j + 1] * x_f[pl.ds(j, B_DEV, stride=TBL), :]
        pg[i] = acc.astype(BF)

    pl.semaphore_wait(barrier, len(partners))
    for dy, dc in group_offsets(False):
        start(head_copy(dy, dc))

    def table(h, d):
        return h * NX + lax.rem(mx + d, NX)

    def a2a(n, dx, dy, dc):
        o = dy * 2 + dc
        rows = pl.ds(*CHUNKS[n])
        return remote(
            send.at[dx, o, rows], recv.at[dx, o, rows], a_s.at[n, dx, o], a_r.at[n, dx, o], peer(dx, dy, dc)
        )

    kpos = iota((LOOK, B_DEV), 0)
    for dx in X_ORDER:
        parts = []
        for h in range(HALVES):
            t = table(h, dx)
            bags = (kpos >= off_v[pl.ds(t, 1), :]) & (kpos < after_v[pl.ds(t, 1), :])
            values = dot(bags.astype(BF), pg[t]).astype(BF)
            parts.append(dot(spread(slot_v[pl.ds(t, 1), :]), values).reshape(GROUPS, CAP, E))
        both = jnp.concatenate(parts, axis=1).astype(BF)
        send[dx] = both
        if dx == 0:
            recv[0, 0] = both[0]
        for dy, dc in a2a_targets(dx):
            start(a2a(0, dx, dy, dc))
    for n in range(1, len(CHUNKS)):
        for dx in X_ORDER:
            for dy, dc in a2a_targets(dx):
                start(a2a(n, dx, dy, dc))

    for dy, dc in group_offsets(False):
        head_copy(dy, dc).wait_recv()
    spots = dot(head_in[...].reshape(GROUPS * HEAD, E), fold).reshape(GROUPS, HEAD, SLOTS)
    got = jnp.sum(spots * mine, axis=0)
    got = got[0:TBL] * 32.0 + got[TBL:2 * TBL] - 1.0
    for q in range(NX):
        tq[q] = jnp.where(iota((8, SLOTS), 0) == 0, got[q:q + 1, :], got[q + NX:q + NX + 1, :])

    def target_copy(dx):
        return remote(tq.at[lax.rem(mx + dx, NX)], tgt.at[dx], t_s.at[dx], t_r.at[dx], peer(dx, 0, 0))

    for dx in X_ORDER[:-1]:
        start(target_copy(dx))
    tgt[0] = tq[mx]

    loads[5].wait()
    order = [(h, d) for h in range(HALVES) for d in range(NX)]
    columns = jnp.swapaxes(
        jnp.concatenate([acc_v[pl.ds(table(h, d), 1), :] for h, d in order], axis=0), 0, 1
    )
    for dx in X_ORDER[:-1]:
        target_copy(dx).wait_recv()

    def scatter(h):
        acc = None
        for dx in X_ORDER:
            for n in range(len(CHUNKS)):
                first = n == h if len(CHUNKS) > 1 else h == 0
                if first:
                    for dy, dc in a2a_targets(dx):
                        a2a(n, dx, dy, dc).wait_recv()
            lo, hi = (0, 32) if h == 0 else (16, 48)
            at = h * CAP - lo
            values = recv[dx, :, lo:hi, :].astype(F32)[:, at:at + CAP, :]
            values = values.reshape(SLOTS, E).astype(BF)
            onehot = (iota((ROWS_DEV, SLOTS), 0) == tgt[dx, h:h + 1, :].astype(I32)).astype(BF)
            part = dot(onehot, values)
            acc = part if acc is None else acc + part
        total[h] = acc
        zs[h] = acc.astype(BF)
        start(*z_reduce(h))

    own_rows = pl.ds(pl.multiple_of(mz * PIECE, PIECE), PIECE)

    def z_reduce(h):
        return [
            remote(
                zs.at[h, pl.ds(pl.multiple_of(lax.rem(mz + d, NZ) * PIECE, PIECE), PIECE)],
                zin.at[h, d], z_s.at[h, d], z_r.at[h, d], z_peer(d),
            )
            for d in Z_ORDER
        ]

    def z_gather(h, d):
        t = table(h, 0)
        return remote(g.at[t, 0], g.at[t, NZ - d], zg_s.at[h, d], zg_r.at[h, d], z_peer(d))

    def x_gather(h, n, dx, d):
        at = g.at[table(h, d), pl.ds(*PARTS[n])]
        return remote(at, at, xg_s.at[h, n, dx], xg_r.at[h, n, dx], peer(dx, 0, 0))

    def z_sum(h):
        acc = total[h, own_rows]
        for d, copy in reversed(list(zip(Z_ORDER, z_reduce(h)))):
            copy.wait_recv()
            acc = acc + zin[h, d].astype(F32)
        g[table(h, 0), 0] = acc.astype(BF)
        start(*[z_gather(h, d) for d in Z_ORDER])
        x_send(h, 0)

    def x_send(h, n):
        first, count = PARTS[n]
        for e in range(first, first + count):
            if e:
                remote(g.at[table(h, 0), 0], g.at[table(h, 0), e], zg_s.at[h, NZ - e], zg_r.at[h, NZ - e], z_peer(e)).wait_recv()
        start(*[x_gather(h, n, dx, 0) for dx in X_ORDER[:-1]])

    fresh = [columns]

    def update(h, d):
        t = table(h, d)
        grad = jnp.concatenate([g[t, lax.rem(w_at - mz + NZ, NZ)] for w_at in range(NZ)], axis=0).astype(F32)
        lane = h * NX + d
        accum = columns[:, lane:lane + 1] + jnp.sum(grad * grad, axis=1, keepdims=True) * (1.0 / E)
        fresh[0] = jnp.where(iota((ROWS_DEV, TBL), 1) == lane, accum, fresh[0])
        out_ref[t] = (grad * (LEARN * lax.rsqrt(accum))).astype(BF)

    def finish(h):
        update(h, 0)
        for dx in (1, 3, 2):
            for n in range(len(PARTS)):
                x_gather(h, n, dx, NX - dx).wait_recv()
            update(h, NX - dx)

    scatter(0)
    scatter(1)
    z_sum(0)
    x_send(0, 1)
    x_send(0, 2)
    z_sum(1)
    x_send(0, 3)
    x_send(1, 1)
    x_send(1, 2)
    finish(0)
    x_send(1, 3)
    finish(1)
    rows = jnp.swapaxes(fresh[0], 0, 1)
    for n, (h, d) in enumerate(order):
        out_accum_ref[pl.ds(table(h, d), 1), :] = rows[n:n + 1, :]
    for copy in sends:
        copy.wait_send()


def row_steps(cot, pooled, w, ids, offsets, accum):
    vmem = pl.BlockSpec(memory_space=pltpu.VMEM)
    anywhere = pl.BlockSpec(memory_space=pl.ANY)
    dma = pltpu.SemaphoreType.DMA
    return pl.pallas_call(
        step_kernel,
        out_shape=(
            jax.ShapeDtypeStruct((TBL, ROWS_DEV, E), BF),
            jax.ShapeDtypeStruct((TBL, ROWS_DEV), F32),
        ),
        in_specs=[anywhere] * 6,
        out_specs=(vmem, vmem),
        scratch_shapes=[
            pltpu.VMEM((B_DEV, TBL * E), BF),
            pltpu.VMEM((B_DEV, TBL, E), BF),
            pltpu.VMEM((B_DEV * TBL, E), F32),
            pltpu.VMEM((TBL * TBL, TBL * E), BF),
            pltpu.VMEM((TBL, LOOK), I32),
            pltpu.VMEM((TBL, B_DEV), I32),
            pltpu.VMEM((TBL, B_DEV), I32),
            pltpu.VMEM((TBL, LOOK), I32),
            pltpu.VMEM((TBL, ROWS_DEV), F32),
            pltpu.VMEM((TBL, B_DEV, E), BF),
            pltpu.VMEM((GROUPS, HEAD, E), BF),
            pltpu.VMEM((GROUPS, HEAD, E), BF),
            pltpu.VMEM((NX, GROUPS, MSG, E), BF),
            pltpu.VMEM((NX, GROUPS, MSG, E), BF),
            pltpu.VMEM((NX, 8, SLOTS), F32),
            pltpu.VMEM((NX, 8, SLOTS), F32),
            pltpu.VMEM((HALVES, ROWS_DEV, E), F32),
            pltpu.VMEM((HALVES, ROWS_DEV, E), BF),
            pltpu.VMEM((HALVES, NZ, PIECE, E), BF),
            pltpu.VMEM((TBL, NZ, PIECE, E), BF),
            dma((6,)),
            dma((GROUPS,)), dma((GROUPS,)),
            dma((len(CHUNKS), NX, GROUPS)), dma((len(CHUNKS), NX, GROUPS)),
            dma((NX,)), dma((NX,)),
            dma((HALVES, NZ)), dma((HALVES, NZ)),
            dma((HALVES, NZ)), dma((HALVES, NZ)),
            dma((HALVES, len(PARTS), NX)), dma((HALVES, len(PARTS), NX)),
        ],
        compiler_params=pltpu.CompilerParams(
            collective_id=0, has_side_effects=True, vmem_limit_bytes=56 * 1024 * 1024
        ),
    )(cot, pooled, w, ids, offsets, accum)


def step(cot, pooled, w, ids, offsets, table, accum):
    delta, new_accum = row_steps(cot, pooled, w, ids, offsets, accum)
    return table - delta.astype(F32), new_accum


def solution(mesh):
    return jax.shard_map(
        step,
        mesh=mesh,
        in_specs=(
            P(("rep", "shard"), None),
            P(("rep", "shard"), None, None),
            P(),
            P(("rep", "shard"), None, None),
            P(("rep", "shard"), None, None),
            P(None, "shard", None),
            P(None, "shard"),
        ),
        out_specs=(P(None, "shard", None), P(None, "shard")),
        check_vma=False,
    )
```

```python
import jax
import jax.numpy as jnp
from jax import lax
from jax.experimental import pallas as pl
from jax.experimental.pallas import tpu as pltpu
from jax.sharding import PartitionSpec as P

LEARN = 0.5
NX, NZ, NY = 4, 12, 8
GROUPS = 2 * NY
TBL, E, B_DEV, LOOK, CAP, ROWS_DEV = 8, 128, 128, 192, 24, 576
SLOTS = GROUPS * CAP
HEAD = 16
HALVES = TBL // NX
MSG = HALVES * CAP
CHUNKS = ((0, 32), (32, 16))
PIECE = ROWS_DEV // NZ
BF, F32, I32 = jnp.bfloat16, jnp.float32, jnp.int32
X_ORDER = (2, 1, 3, 0)
Y_ORDER = (4, 3, 5, 2, 6, 1, 7, 0)
Z_ORDER = (1, 11, 2, 10, 3, 9, 4, 8, 5, 7, 6)
PARTS = ((0, 1), (1, 3), (9, 3), (4, 5))


def iota(shape, dim):
    return lax.broadcasted_iota(I32, shape, dim)


def dot(a, b, dims=((1,), (0,))):
    return lax.dot_general(a, b, (dims, ((), ())), preferred_element_type=F32)


def group_offsets(own):
    return [(dy, dc) for dy in Y_ORDER for dc in (0, 1) if own or (dy, dc) != (0, 0)]


def remote(src, dst, s, r, peer):
    return pltpu.make_async_remote_copy(
        src, dst, s, r, device_id=peer, device_id_type=pl.DeviceIdType.MESH
    )


def step_kernel(
    cot_hbm, x_hbm, w_hbm, ids_hbm, off_hbm, accum_hbm,
    out_hbm, out_accum_hbm,
    cot, x_in, x_f, w_v, ids_v, off_v, after_v, slot_v, acc_v, pg,
    head_out, head_in, send, recv, tq, tgt, total, zs, zin, g,
    load_sem, hd_s, hd_r, a_s, a_r, t_s, t_r, z_s, z_r, zg_s, zg_r, xg_s, xg_r, out_ref, fresh_v, out_sem, fresh_sem,
):
    rep = lax.axis_index("rep")
    sh = lax.axis_index("shard")
    mx, mz = rep // NZ, rep % NZ
    my, mc = sh // 2, sh % 2

    def peer(dx, dy, dc):
        return {
            "rep": lax.rem(mx + dx, NX) * NZ + mz,
            "shard": lax.rem(my + dy, NY) * 2 + lax.rem(mc + dc, 2),
        }

    def z_peer(d):
        return {"rep": mx * NZ + lax.rem(mz + d, NZ), "shard": sh}

    def a2a_targets(dx):
        return [(dy, dc) for dy, dc in group_offsets(dx != 0)]

    loads = [
        pltpu.make_async_copy(src, dst, load_sem.at[n])
        for n, (src, dst) in enumerate(
            (
                (ids_hbm.at[0], ids_v), (off_hbm.at[0], off_v), (cot_hbm, cot), (w_hbm, w_v),
                (x_hbm, x_in), (accum_hbm, acc_v),
            )
        )
    ]
    for copy in loads:
        copy.start()

    barrier = pltpu.get_barrier_semaphore()
    partners = [peer(dx, dy, dc) for dx in X_ORDER for dy, dc in a2a_targets(dx)]
    partners += [z_peer(d) for d in range(1, NZ)]
    for other in partners:
        pl.semaphore_signal(barrier, inc=1, device_id=other, device_id_type=pl.DeviceIdType.MESH)
    sends = []

    def start(*copies):
        for copy in copies:
            copy.start()
            sends.append(copy)

    loads[0].wait()
    loads[1].wait()
    ids = ids_v[...]
    owner = lax.shift_right_logical(ids * 7282, 22)
    local = ids - owner * ROWS_DEV + 1
    rel = ((lax.shift_right_logical(owner, 1) - my) & (NY - 1)) * 2 + ((owner & 1) ^ mc)
    member = jnp.concatenate(
        [(rel[t:t + 1, :] == iota((GROUPS, LOOK), 0)).astype(F32) for t in range(TBL)], axis=0
    )
    earlier = (iota((LOOK, LOOK), 0) < iota((LOOK, LOOK), 1)).astype(BF)
    before = dot(member.astype(BF), earlier)
    rank = jnp.sum((member * before).reshape(TBL, GROUPS, LOOK), axis=1).astype(I32)
    slot = rel * CAP + rank
    slot_v[...] = slot
    high = lax.shift_right_logical(local, 5).astype(F32)
    low = (local & 31).astype(F32)
    after = pltpu.roll(off_v[...], B_DEV - 1, 1)
    after_v[...] = jnp.where(iota((TBL, B_DEV), 1) == B_DEV - 1, LOOK, after)

    def spread(row):
        return (iota((SLOTS, LOOK), 0) == row).astype(BF)

    rows_h, rows_l = [], []
    for t in range(TBL):
        hl = jnp.where(iota((8, LOOK), 0) == 0, high[t:t + 1, :], low[t:t + 1, :]).astype(BF)
        placed = dot(hl, spread(slot[t:t + 1, :]), ((1,), (1,)))
        rows_h.append(placed[0:1, :])
        rows_l.append(placed[1:2, :])
    targets = jnp.concatenate(rows_h + rows_l, axis=0)
    mine = (iota((GROUPS, 1, SLOTS), 2) // CAP == iota((GROUPS, 1, SLOTS), 0)).astype(F32)
    fold = (iota((E, SLOTS), 1) % CAP == iota((E, SLOTS), 0)).astype(BF)
    apart = (targets[None] * mine).astype(BF).reshape(GROUPS * HEAD, SLOTS)
    heads = dot(apart, fold, ((1,), (1,))).astype(BF).reshape(GROUPS, HEAD, E)
    head_out[...] = heads
    head_in[0] = heads[0]

    def head_copy(dy, dc):
        o = dy * 2 + dc
        return remote(head_out.at[o], head_in.at[o], hd_s.at[o], hd_r.at[o], peer(0, dy, dc))

    swap = (iota((64, 64), 1) == (iota((64, 64), 0) % 8) * 8 + iota((64, 64), 0) // 8).astype(BF)
    loads[2].wait()
    loads[3].wait()
    w = w_v[...]
    w_t = dot(swap, w).astype(BF)
    sym = dot(cot[...], w, ((1,), (1,))) + dot(cot[...], w_t, ((1,), (1,)))
    loads[4].wait()
    x_f[...] = x_in[...].astype(F32).reshape(B_DEV * TBL, E)
    for i in range(TBL):
        acc = cot[:, i * E:(i + 1) * E].astype(F32)
        for j in range(TBL):
            acc = acc + sym[:, i * TBL + j:i * TBL + j + 1] * x_f[pl.ds(j, B_DEV, stride=TBL), :]
        pg[i] = acc.astype(BF)

    pl.semaphore_wait(barrier, len(partners))
    for dy, dc in group_offsets(False):
        start(head_copy(dy, dc))

    def table(h, d):
        return h * NX + lax.rem(mx + d, NX)

    def a2a(n, dx, dy, dc):
        o = dy * 2 + dc
        rows = pl.ds(*CHUNKS[n])
        return remote(
            send.at[dx, o, rows], recv.at[dx, o, rows], a_s.at[n, dx, o], a_r.at[n, dx, o], peer(dx, dy, dc)
        )

    kpos = iota((LOOK, B_DEV), 0)
    for dx in X_ORDER:
        parts = []
        for h in range(HALVES):
            t = table(h, dx)
            bags = (kpos >= off_v[pl.ds(t, 1), :]) & (kpos < after_v[pl.ds(t, 1), :])
            values = dot(bags.astype(BF), pg[t]).astype(BF)
            parts.append(dot(spread(slot_v[pl.ds(t, 1), :]), values).reshape(GROUPS, CAP, E))
        both = jnp.concatenate(parts, axis=1).astype(BF)
        send[dx] = both
        if dx == 0:
            recv[0, 0] = both[0]
        for dy, dc in a2a_targets(dx):
            start(a2a(0, dx, dy, dc))
    for n in range(1, len(CHUNKS)):
        for dx in X_ORDER:
            for dy, dc in a2a_targets(dx):
                start(a2a(n, dx, dy, dc))

    for dy, dc in group_offsets(False):
        head_copy(dy, dc).wait_recv()
    spots = dot(head_in[...].reshape(GROUPS * HEAD, E), fold).reshape(GROUPS, HEAD, SLOTS)
    got = jnp.sum(spots * mine, axis=0)
    got = got[0:TBL] * 32.0 + got[TBL:2 * TBL] - 1.0
    for q in range(NX):
        tq[q] = jnp.where(iota((8, SLOTS), 0) == 0, got[q:q + 1, :], got[q + NX:q + NX + 1, :])

    def target_copy(dx):
        return remote(tq.at[lax.rem(mx + dx, NX)], tgt.at[dx], t_s.at[dx], t_r.at[dx], peer(dx, 0, 0))

    for dx in X_ORDER[:-1]:
        start(target_copy(dx))
    tgt[0] = tq[mx]

    loads[5].wait()
    order = [(h, d) for h in range(HALVES) for d in range(NX)]
    columns = jnp.swapaxes(
        jnp.concatenate([acc_v[pl.ds(table(h, d), 1), :] for h, d in order], axis=0), 0, 1
    )
    for dx in X_ORDER[:-1]:
        target_copy(dx).wait_recv()

    def scatter(h):
        acc = None
        for dx in X_ORDER:
            for n in range(len(CHUNKS)):
                first = n == h if len(CHUNKS) > 1 else h == 0
                if first:
                    for dy, dc in a2a_targets(dx):
                        a2a(n, dx, dy, dc).wait_recv()
            lo, hi = (0, 32) if h == 0 else (16, 48)
            at = h * CAP - lo
            values = recv[dx, :, lo:hi, :].astype(F32)[:, at:at + CAP, :]
            values = values.reshape(SLOTS, E).astype(BF)
            onehot = (iota((ROWS_DEV, SLOTS), 0) == tgt[dx, h:h + 1, :].astype(I32)).astype(BF)
            part = dot(onehot, values)
            acc = part if acc is None else acc + part
        total[h] = acc
        zs[h] = acc.astype(BF)
        start(*z_reduce(h))

    own_rows = pl.ds(pl.multiple_of(mz * PIECE, PIECE), PIECE)

    def z_reduce(h):
        return [
            remote(
                zs.at[h, pl.ds(pl.multiple_of(lax.rem(mz + d, NZ) * PIECE, PIECE), PIECE)],
                zin.at[h, d], z_s.at[h, d], z_r.at[h, d], z_peer(d),
            )
            for d in Z_ORDER
        ]

    def z_gather(h, d):
        t = table(h, 0)
        return remote(g.at[t, 0], g.at[t, NZ - d], zg_s.at[h, d], zg_r.at[h, d], z_peer(d))

    def x_gather(h, n, dx, d):
        at = g.at[table(h, d), pl.ds(*PARTS[n])]
        return remote(at, at, xg_s.at[h, n, dx], xg_r.at[h, n, dx], peer(dx, 0, 0))

    def z_sum(h):
        acc = total[h, own_rows]
        for d, copy in list(zip(Z_ORDER, z_reduce(h))):
            copy.wait_recv()
            acc = acc + zin[h, d].astype(F32)
        g[table(h, 0), 0] = acc.astype(BF)
        start(*[z_gather(h, d) for d in Z_ORDER])
        x_send(h, 0)

    def x_send(h, n):
        first, count = PARTS[n]
        for e in range(first, first + count):
            if e:
                remote(g.at[table(h, 0), 0], g.at[table(h, 0), e], zg_s.at[h, NZ - e], zg_r.at[h, NZ - e], z_peer(e)).wait_recv()
        start(*[x_gather(h, n, dx, 0) for dx in X_ORDER[:-1]])

    fresh, stores = [columns], []

    def update(h, d):
        t = table(h, d)
        grad = jnp.concatenate([g[t, lax.rem(w_at - mz + NZ, NZ)] for w_at in range(NZ)], axis=0).astype(F32)
        lane = h * NX + d
        accum = columns[:, lane:lane + 1] + jnp.sum(grad * grad, axis=1, keepdims=True) * (1.0 / E)
        fresh[0] = jnp.where(iota((ROWS_DEV, TBL), 1) == lane, accum, fresh[0])
        out_ref[t] = (grad * (LEARN * lax.rsqrt(accum))).astype(BF)
        store = pltpu.make_async_copy(out_ref.at[t], out_hbm.at[t], out_sem.at[lane])
        store.start()
        stores.append(store)

    def finish(h):
        for dx in (1, 3, 2):
            for n in range(len(PARTS)):
                x_gather(h, n, dx, NX - dx).wait_recv()
            update(h, NX - dx)

    scatter(0)
    scatter(1)
    z_sum(0)
    x_send(0, 1)
    x_send(0, 2)
    z_sum(1)
    x_send(0, 3)
    x_send(1, 1)
    x_send(1, 2)
    update(0, 0)
    finish(0)
    x_send(1, 3)
    update(1, 0)
    finish(1)
    rows = jnp.swapaxes(fresh[0], 0, 1)
    for n, (h, d) in enumerate(order):
        fresh_v[pl.ds(table(h, d), 1), :] = rows[n:n + 1, :]
    stores.append(pltpu.make_async_copy(fresh_v, out_accum_hbm, fresh_sem))
    stores[-1].start()
    for copy in sends:
        copy.wait_send()
    for store in stores:
        store.wait()


def row_steps(cot, pooled, w, ids, offsets, accum):
    anywhere = pl.BlockSpec(memory_space=pl.ANY)
    dma = pltpu.SemaphoreType.DMA
    return pl.pallas_call(
        step_kernel,
        out_shape=(
            jax.ShapeDtypeStruct((TBL, ROWS_DEV, E), BF),
            jax.ShapeDtypeStruct((TBL, ROWS_DEV), F32),
        ),
        in_specs=[anywhere] * 6,
        out_specs=(anywhere, anywhere),
        scratch_shapes=[
            pltpu.VMEM((B_DEV, TBL * E), BF),
            pltpu.VMEM((B_DEV, TBL, E), BF),
            pltpu.VMEM((B_DEV * TBL, E), F32),
            pltpu.VMEM((TBL * TBL, TBL * E), BF),
            pltpu.VMEM((TBL, LOOK), I32),
            pltpu.VMEM((TBL, B_DEV), I32),
            pltpu.VMEM((TBL, B_DEV), I32),
            pltpu.VMEM((TBL, LOOK), I32),
            pltpu.VMEM((TBL, ROWS_DEV), F32),
            pltpu.VMEM((TBL, B_DEV, E), BF),
            pltpu.VMEM((GROUPS, HEAD, E), BF),
            pltpu.VMEM((GROUPS, HEAD, E), BF),
            pltpu.VMEM((NX, GROUPS, MSG, E), BF),
            pltpu.VMEM((NX, GROUPS, MSG, E), BF),
            pltpu.VMEM((NX, 8, SLOTS), F32),
            pltpu.VMEM((NX, 8, SLOTS), F32),
            pltpu.VMEM((HALVES, ROWS_DEV, E), F32),
            pltpu.VMEM((HALVES, ROWS_DEV, E), BF),
            pltpu.VMEM((HALVES, NZ, PIECE, E), BF),
            pltpu.VMEM((TBL, NZ, PIECE, E), BF),
            dma((6,)),
            dma((GROUPS,)), dma((GROUPS,)),
            dma((len(CHUNKS), NX, GROUPS)), dma((len(CHUNKS), NX, GROUPS)),
            dma((NX,)), dma((NX,)),
            dma((HALVES, NZ)), dma((HALVES, NZ)),
            dma((HALVES, NZ)), dma((HALVES, NZ)),
            dma((HALVES, len(PARTS), NX)), dma((HALVES, len(PARTS), NX)),
            pltpu.VMEM((TBL, ROWS_DEV, E), BF), pltpu.VMEM((TBL, ROWS_DEV), F32),
            dma((TBL,)), dma,
        ],
        compiler_params=pltpu.CompilerParams(
            collective_id=0, has_side_effects=True, vmem_limit_bytes=56 * 1024 * 1024
        ),
    )(cot, pooled, w, ids, offsets, accum)


def apply_kernel(
    delta_hbm, table_hbm, accum_hbm, new_table_hbm, new_accum_hbm,
    delta, tab, acc_v, d_sem, t_sem, o_sem, a_sem,
):
    acc_in = pltpu.make_async_copy(accum_hbm, acc_v, a_sem.at[0])
    acc_out = pltpu.make_async_copy(acc_v, new_accum_hbm, a_sem.at[1])
    stores = []
    acc_in.start()
    loads = []
    for t in range(TBL):
        pair = (
            pltpu.make_async_copy(delta_hbm.at[t], delta.at[t], d_sem.at[t]),
            pltpu.make_async_copy(table_hbm.at[t], tab.at[t], t_sem.at[t]),
        )
        for copy in pair:
            copy.start()
        loads.append(pair)
    acc_in.wait()
    acc_out.start()
    for t in range(TBL):
        for copy in loads[t]:
            copy.wait()
        tab[t] = tab[t] - delta[t].astype(F32)
        store = pltpu.make_async_copy(tab.at[t], new_table_hbm.at[t], o_sem.at[t])
        store.start()
        stores.append(store)
    acc_out.wait()
    for store in stores:
        store.wait()


def step(cot, pooled, w, ids, offsets, table, accum):
    delta, new_accum = row_steps(cot, pooled, w, ids, offsets, accum)
    anywhere = pl.BlockSpec(memory_space=pl.ANY)
    dma = pltpu.SemaphoreType.DMA
    return pl.pallas_call(
        apply_kernel,
        out_shape=(
            jax.ShapeDtypeStruct((TBL, ROWS_DEV, E), F32),
            jax.ShapeDtypeStruct((TBL, ROWS_DEV), F32),
        ),
        in_specs=[anywhere] * 3,
        out_specs=(anywhere, anywhere),
        scratch_shapes=[
            pltpu.VMEM((TBL, ROWS_DEV, E), BF),
            pltpu.VMEM((TBL, ROWS_DEV, E), F32),
            pltpu.VMEM((TBL, ROWS_DEV), F32),
            dma((TBL,)), dma((TBL,)), dma((TBL,)), dma((2,)),
        ],
        compiler_params=pltpu.CompilerParams(vmem_limit_bytes=56 * 1024 * 1024),
    )(delta, table, new_accum)


def solution(mesh):
    return jax.shard_map(
        step,
        mesh=mesh,
        in_specs=(
            P(("rep", "shard"), None),
            P(("rep", "shard"), None, None),
            P(),
            P(("rep", "shard"), None, None),
            P(("rep", "shard"), None, None),
            P(None, "shard", None),
            P(None, "shard"),
        ),
        out_specs=(P(None, "shard", None), P(None, "shard")),
        check_vma=False,
    )
```

```python
import jax
import jax.numpy as jnp
from jax import lax
from jax.experimental import pallas as pl
from jax.experimental.pallas import tpu as pltpu
from jax.sharding import PartitionSpec as P

LEARN = 0.5
NX, NZ, NY = 4, 12, 8
GROUPS = 2 * NY
TBL, E, B_DEV, LOOK, CAP, ROWS_DEV = 8, 128, 128, 192, 24, 576
SLOTS = GROUPS * CAP
HEAD = 16
HALVES = TBL // NX
MSG = HALVES * CAP
CHUNKS = ((0, 32), (32, 16))
PIECE = ROWS_DEV // NZ
BF, F32, I32 = jnp.bfloat16, jnp.float32, jnp.int32
X_ORDER = (2, 1, 3, 0)
Y_ORDER = (4, 3, 5, 2, 6, 1, 7, 0)
Z_ORDER = (1, 11, 2, 10, 3, 9, 4, 8, 5, 7, 6)
PARTS = ((0, 1), (1, 3), (9, 3), (4, 5))


def iota(shape, dim):
    return lax.broadcasted_iota(I32, shape, dim)


def dot(a, b, dims=((1,), (0,))):
    return lax.dot_general(a, b, (dims, ((), ())), preferred_element_type=F32)


def group_offsets(own):
    return [(dy, dc) for dy in Y_ORDER for dc in (0, 1) if own or (dy, dc) != (0, 0)]


def remote(src, dst, s, r, peer):
    return pltpu.make_async_remote_copy(
        src, dst, s, r, device_id=peer, device_id_type=pl.DeviceIdType.MESH
    )


def step_kernel(
    cot_hbm, x_hbm, w_hbm, ids_hbm, off_hbm, accum_hbm,
    out_hbm, out_accum_hbm,
    cot, x_in, x_f, w_v, ids_v, off_v, after_v, slot_v, acc_v, pg,
    head_out, head_in, send, recv, tq, tgt, total, zs, zin, g,
    load_sem, hd_s, hd_r, a_s, a_r, t_s, t_r, z_s, z_r, zg_s, zg_r, xg_s, xg_r, out_ref, fresh_v, out_sem, fresh_sem,
):
    rep = lax.axis_index("rep")
    sh = lax.axis_index("shard")
    mx, mz = rep // NZ, rep % NZ
    my, mc = sh // 2, sh % 2

    def peer(dx, dy, dc):
        return {
            "rep": lax.rem(mx + dx, NX) * NZ + mz,
            "shard": lax.rem(my + dy, NY) * 2 + lax.rem(mc + dc, 2),
        }

    def z_peer(d):
        return {"rep": mx * NZ + lax.rem(mz + d, NZ), "shard": sh}

    def a2a_targets(dx):
        return [(dy, dc) for dy, dc in group_offsets(dx != 0)]

    loads = [
        pltpu.make_async_copy(src, dst, load_sem.at[n])
        for n, (src, dst) in enumerate(
            (
                (ids_hbm.at[0], ids_v), (off_hbm.at[0], off_v), (cot_hbm, cot), (w_hbm, w_v),
                (x_hbm, x_in), (accum_hbm, acc_v),
            )
        )
    ]
    for copy in loads:
        copy.start()

    barrier = pltpu.get_barrier_semaphore()
    ranked = [
        (min(dx, NX - dx) + min(dy, NY - dy), dx, dy, dc) for dx in X_ORDER for dy, dc in a2a_targets(dx)
    ]
    ranked += [(min(d, NZ - d), d) for d in range(1, NZ)]
    ranked.sort(key=lambda entry: -entry[0])
    partners = [z_peer(entry[1]) if len(entry) == 2 else peer(*entry[1:]) for entry in ranked]
    for other in partners:
        pl.semaphore_signal(barrier, inc=1, device_id=other, device_id_type=pl.DeviceIdType.MESH)
    sends = []

    def start(*copies):
        for copy in copies:
            copy.start()
            sends.append(copy)

    loads[0].wait()
    loads[1].wait()
    ids = ids_v[...]
    owner = lax.shift_right_logical(ids * 7282, 22)
    local = ids - owner * ROWS_DEV + 1
    rel = ((lax.shift_right_logical(owner, 1) - my) & (NY - 1)) * 2 + ((owner & 1) ^ mc)
    member = jnp.concatenate(
        [(rel[t:t + 1, :] == iota((GROUPS, LOOK), 0)).astype(F32) for t in range(TBL)], axis=0
    )
    earlier = (iota((LOOK, LOOK), 0) < iota((LOOK, LOOK), 1)).astype(BF)
    before = dot(member.astype(BF), earlier)
    rank = jnp.sum((member * before).reshape(TBL, GROUPS, LOOK), axis=1).astype(I32)
    slot = rel * CAP + rank
    slot_v[...] = slot
    high = lax.shift_right_logical(local, 5).astype(F32)
    low = (local & 31).astype(F32)
    after = pltpu.roll(off_v[...], B_DEV - 1, 1)
    after_v[...] = jnp.where(iota((TBL, B_DEV), 1) == B_DEV - 1, LOOK, after)

    def spread(row):
        return (iota((SLOTS, LOOK), 0) == row).astype(BF)

    rows_h, rows_l = [], []
    for t in range(TBL):
        hl = jnp.where(iota((8, LOOK), 0) == 0, high[t:t + 1, :], low[t:t + 1, :]).astype(BF)
        placed = dot(hl, spread(slot[t:t + 1, :]), ((1,), (1,)))
        rows_h.append(placed[0:1, :])
        rows_l.append(placed[1:2, :])
    targets = jnp.concatenate(rows_h + rows_l, axis=0)
    mine = (iota((GROUPS, 1, SLOTS), 2) // CAP == iota((GROUPS, 1, SLOTS), 0)).astype(F32)
    fold = (iota((E, SLOTS), 1) % CAP == iota((E, SLOTS), 0)).astype(BF)
    apart = (targets[None] * mine).astype(BF).reshape(GROUPS * HEAD, SLOTS)
    heads = dot(apart, fold, ((1,), (1,))).astype(BF).reshape(GROUPS, HEAD, E)
    head_out[...] = heads
    head_in[0] = heads[0]

    def head_copy(dy, dc):
        o = dy * 2 + dc
        return remote(head_out.at[o], head_in.at[o], hd_s.at[o], hd_r.at[o], peer(0, dy, dc))

    swap = (iota((64, 64), 1) == (iota((64, 64), 0) % 8) * 8 + iota((64, 64), 0) // 8).astype(BF)
    loads[2].wait()
    loads[3].wait()
    w = w_v[...]
    w_t = dot(swap, w).astype(BF)
    sym = dot(cot[...], w, ((1,), (1,))) + dot(cot[...], w_t, ((1,), (1,)))
    loads[4].wait()
    x_f[...] = x_in[...].astype(F32).reshape(B_DEV * TBL, E)
    for i in range(TBL):
        acc = cot[:, i * E:(i + 1) * E].astype(F32)
        for j in range(TBL):
            acc = acc + sym[:, i * TBL + j:i * TBL + j + 1] * x_f[pl.ds(j, B_DEV, stride=TBL), :]
        pg[i] = acc.astype(BF)

    pl.semaphore_wait(barrier, len(partners))
    for dy, dc in group_offsets(False):
        start(head_copy(dy, dc))

    def table(h, d):
        return h * NX + lax.rem(mx + d, NX)

    def a2a(n, dx, dy, dc):
        o = dy * 2 + dc
        rows = pl.ds(*CHUNKS[n])
        return remote(
            send.at[dx, o, rows], recv.at[dx, o, rows], a_s.at[n, dx, o], a_r.at[n, dx, o], peer(dx, dy, dc)
        )

    kpos = iota((LOOK, B_DEV), 0)
    for dx in X_ORDER:
        parts = []
        for h in range(HALVES):
            t = table(h, dx)
            bags = (kpos >= off_v[pl.ds(t, 1), :]) & (kpos < after_v[pl.ds(t, 1), :])
            values = dot(bags.astype(BF), pg[t]).astype(BF)
            parts.append(dot(spread(slot_v[pl.ds(t, 1), :]), values).reshape(GROUPS, CAP, E))
        both = jnp.concatenate(parts, axis=1).astype(BF)
        send[dx] = both
        if dx == 0:
            recv[0, 0] = both[0]
        for dy, dc in a2a_targets(dx):
            start(a2a(0, dx, dy, dc))
    for n in range(1, len(CHUNKS)):
        for dx in X_ORDER:
            for dy, dc in a2a_targets(dx):
                start(a2a(n, dx, dy, dc))

    for dy, dc in group_offsets(False):
        head_copy(dy, dc).wait_recv()
    spots = dot(head_in[...].reshape(GROUPS * HEAD, E), fold).reshape(GROUPS, HEAD, SLOTS)
    got = jnp.sum(spots * mine, axis=0)
    got = got[0:TBL] * 32.0 + got[TBL:2 * TBL] - 1.0
    for q in range(NX):
        tq[q] = jnp.where(iota((8, SLOTS), 0) == 0, got[q:q + 1, :], got[q + NX:q + NX + 1, :])

    def target_copy(dx):
        return remote(tq.at[lax.rem(mx + dx, NX)], tgt.at[dx], t_s.at[dx], t_r.at[dx], peer(dx, 0, 0))

    for dx in X_ORDER[:-1]:
        start(target_copy(dx))
    tgt[0] = tq[mx]

    loads[5].wait()
    order = [(h, d) for h in range(HALVES) for d in range(NX)]
    columns = jnp.swapaxes(
        jnp.concatenate([acc_v[pl.ds(table(h, d), 1), :] for h, d in order], axis=0), 0, 1
    )
    for dx in X_ORDER[:-1]:
        target_copy(dx).wait_recv()

    def scatter(h):
        acc = None
        for dx in X_ORDER:
            for n in range(len(CHUNKS)):
                first = n == h if len(CHUNKS) > 1 else h == 0
                if first:
                    for dy, dc in a2a_targets(dx):
                        a2a(n, dx, dy, dc).wait_recv()
            lo, hi = (0, 32) if h == 0 else (16, 48)
            at = h * CAP - lo
            values = recv[dx, :, lo:hi, :].astype(F32)[:, at:at + CAP, :]
            values = values.reshape(SLOTS, E).astype(BF)
            onehot = (iota((ROWS_DEV, SLOTS), 0) == tgt[dx, h:h + 1, :].astype(I32)).astype(BF)
            part = dot(onehot, values)
            acc = part if acc is None else acc + part
        total[h] = acc
        zs[h] = acc.astype(BF)
        start(*z_reduce(h))

    own_rows = pl.ds(pl.multiple_of(mz * PIECE, PIECE), PIECE)

    def z_reduce(h):
        return [
            remote(
                zs.at[h, pl.ds(pl.multiple_of(lax.rem(mz + d, NZ) * PIECE, PIECE), PIECE)],
                zin.at[h, d], z_s.at[h, d], z_r.at[h, d], z_peer(d),
            )
            for d in Z_ORDER
        ]

    def z_gather(h, d):
        t = table(h, 0)
        return remote(g.at[t, 0], g.at[t, NZ - d], zg_s.at[h, d], zg_r.at[h, d], z_peer(d))

    def x_gather(h, n, dx, d):
        at = g.at[table(h, d), pl.ds(*PARTS[n])]
        return remote(at, at, xg_s.at[h, n, dx], xg_r.at[h, n, dx], peer(dx, 0, 0))

    def z_sum(h):
        acc = total[h, own_rows]
        for d, copy in list(zip(Z_ORDER, z_reduce(h))):
            copy.wait_recv()
            acc = acc + zin[h, d].astype(F32)
        g[table(h, 0), 0] = acc.astype(BF)
        start(*[z_gather(h, d) for d in Z_ORDER])
        x_send(h, 0)

    def x_send(h, n):
        first, count = PARTS[n]
        for e in range(first, first + count):
            if e:
                remote(g.at[table(h, 0), 0], g.at[table(h, 0), e], zg_s.at[h, NZ - e], zg_r.at[h, NZ - e], z_peer(e)).wait_recv()
        start(*[x_gather(h, n, dx, 0) for dx in X_ORDER[:-1]])

    fresh, stores = [columns], []

    def update(h, d):
        t = table(h, d)
        grad = jnp.concatenate([g[t, lax.rem(w_at - mz + NZ, NZ)] for w_at in range(NZ)], axis=0).astype(F32)
        lane = h * NX + d
        accum = columns[:, lane:lane + 1] + jnp.sum(grad * grad, axis=1, keepdims=True) * (1.0 / E)
        fresh[0] = jnp.where(iota((ROWS_DEV, TBL), 1) == lane, accum, fresh[0])
        out_ref[t] = (grad * (LEARN * lax.rsqrt(accum))).astype(BF)
        store = pltpu.make_async_copy(out_ref.at[t], out_hbm.at[t], out_sem.at[lane])
        store.start()
        stores.append(store)

    def finish(h):
        for dx in (1, 3, 2):
            for n in range(len(PARTS)):
                x_gather(h, n, dx, NX - dx).wait_recv()
            update(h, NX - dx)

    scatter(0)
    scatter(1)
    z_sum(0)
    x_send(0, 1)
    x_send(0, 2)
    z_sum(1)
    x_send(0, 3)
    x_send(1, 1)
    x_send(1, 2)
    update(0, 0)
    finish(0)
    x_send(1, 3)
    update(1, 0)
    finish(1)
    rows = jnp.swapaxes(fresh[0], 0, 1)
    for n, (h, d) in enumerate(order):
        fresh_v[pl.ds(table(h, d), 1), :] = rows[n:n + 1, :]
    stores.append(pltpu.make_async_copy(fresh_v, out_accum_hbm, fresh_sem))
    stores[-1].start()
    for copy in sends:
        copy.wait_send()
    for store in stores:
        store.wait()


def row_steps(cot, pooled, w, ids, offsets, accum):
    anywhere = pl.BlockSpec(memory_space=pl.ANY)
    dma = pltpu.SemaphoreType.DMA
    return pl.pallas_call(
        step_kernel,
        out_shape=(
            jax.ShapeDtypeStruct((TBL, ROWS_DEV, E), BF),
            jax.ShapeDtypeStruct((TBL, ROWS_DEV), F32),
        ),
        in_specs=[anywhere] * 6,
        out_specs=(anywhere, anywhere),
        scratch_shapes=[
            pltpu.VMEM((B_DEV, TBL * E), BF),
            pltpu.VMEM((B_DEV, TBL, E), BF),
            pltpu.VMEM((B_DEV * TBL, E), F32),
            pltpu.VMEM((TBL * TBL, TBL * E), BF),
            pltpu.VMEM((TBL, LOOK), I32),
            pltpu.VMEM((TBL, B_DEV), I32),
            pltpu.VMEM((TBL, B_DEV), I32),
            pltpu.VMEM((TBL, LOOK), I32),
            pltpu.VMEM((TBL, ROWS_DEV), F32),
            pltpu.VMEM((TBL, B_DEV, E), BF),
            pltpu.VMEM((GROUPS, HEAD, E), BF),
            pltpu.VMEM((GROUPS, HEAD, E), BF),
            pltpu.VMEM((NX, GROUPS, MSG, E), BF),
            pltpu.VMEM((NX, GROUPS, MSG, E), BF),
            pltpu.VMEM((NX, 8, SLOTS), F32),
            pltpu.VMEM((NX, 8, SLOTS), F32),
            pltpu.VMEM((HALVES, ROWS_DEV, E), F32),
            pltpu.VMEM((HALVES, ROWS_DEV, E), BF),
            pltpu.VMEM((HALVES, NZ, PIECE, E), BF),
            pltpu.VMEM((TBL, NZ, PIECE, E), BF),
            dma((6,)),
            dma((GROUPS,)), dma((GROUPS,)),
            dma((len(CHUNKS), NX, GROUPS)), dma((len(CHUNKS), NX, GROUPS)),
            dma((NX,)), dma((NX,)),
            dma((HALVES, NZ)), dma((HALVES, NZ)),
            dma((HALVES, NZ)), dma((HALVES, NZ)),
            dma((HALVES, len(PARTS), NX)), dma((HALVES, len(PARTS), NX)),
            pltpu.VMEM((TBL, ROWS_DEV, E), BF), pltpu.VMEM((TBL, ROWS_DEV), F32),
            dma((TBL,)), dma,
        ],
        compiler_params=pltpu.CompilerParams(
            collective_id=0, has_side_effects=True, vmem_limit_bytes=56 * 1024 * 1024
        ),
    )(cot, pooled, w, ids, offsets, accum)


def apply_kernel(
    delta_hbm, table_hbm, accum_hbm, new_table_hbm, new_accum_hbm,
    delta, tab, acc_v, d_sem, t_sem, o_sem, a_sem,
):
    acc_in = pltpu.make_async_copy(accum_hbm, acc_v, a_sem.at[0])
    acc_out = pltpu.make_async_copy(acc_v, new_accum_hbm, a_sem.at[1])
    stores = []
    acc_in.start()
    loads = []
    for t in range(TBL):
        pair = (
            pltpu.make_async_copy(delta_hbm.at[t], delta.at[t], d_sem.at[t]),
            pltpu.make_async_copy(table_hbm.at[t], tab.at[t], t_sem.at[t]),
        )
        for copy in pair:
            copy.start()
        loads.append(pair)
    acc_in.wait()
    acc_out.start()
    for t in range(TBL):
        for copy in loads[t]:
            copy.wait()
        tab[t] = tab[t] - delta[t].astype(F32)
        store = pltpu.make_async_copy(tab.at[t], new_table_hbm.at[t], o_sem.at[t])
        store.start()
        stores.append(store)
    acc_out.wait()
    for store in stores:
        store.wait()


def step(cot, pooled, w, ids, offsets, table, accum):
    delta, new_accum = row_steps(cot, pooled, w, ids, offsets, accum)
    anywhere = pl.BlockSpec(memory_space=pl.ANY)
    dma = pltpu.SemaphoreType.DMA
    return pl.pallas_call(
        apply_kernel,
        out_shape=(
            jax.ShapeDtypeStruct((TBL, ROWS_DEV, E), F32),
            jax.ShapeDtypeStruct((TBL, ROWS_DEV), F32),
        ),
        in_specs=[anywhere] * 3,
        out_specs=(anywhere, anywhere),
        scratch_shapes=[
            pltpu.VMEM((TBL, ROWS_DEV, E), BF),
            pltpu.VMEM((TBL, ROWS_DEV, E), F32),
            pltpu.VMEM((TBL, ROWS_DEV), F32),
            dma((TBL,)), dma((TBL,)), dma((TBL,)), dma((2,)),
        ],
        compiler_params=pltpu.CompilerParams(vmem_limit_bytes=56 * 1024 * 1024),
    )(delta, table, new_accum)


def solution(mesh):
    return jax.shard_map(
        step,
        mesh=mesh,
        in_specs=(
            P(("rep", "shard"), None),
            P(("rep", "shard"), None, None),
            P(),
            P(("rep", "shard"), None, None),
            P(("rep", "shard"), None, None),
            P(None, "shard", None),
            P(None, "shard"),
        ),
        out_specs=(P(None, "shard", None), P(None, "shard")),
        check_vma=False,
    )
```
